32 devices in a mesh: ctx: 16 (over z, x, core), shard: 2 (over y).
Axes of the slice: x: 2, y: 2, z: 4, core: 2. Of those that a mesh axis runs over, the one named last changes fastest.
Arguments:
- tokens: bfloat16 [2, 4096, 1024], P('shard', 'ctx'), may hold values from -6 to 6
- ln1_gain: bfloat16 [1024], P('shard'), may hold values from 0.25 to 1.75
- ln1_bias: bfloat16 [1024], P('shard'), may hold values from -4 to 4
- qkv_weight: bfloat16 [1024, 3072], P('shard'), may hold values from -0.25 to 0.25
- query_bias: bfloat16 [1024], P('shard'), may hold values from -4 to 4
- value_bias: bfloat16 [1024], P('shard'), may hold values from -4 to 4
- dense_weight: bfloat16 [1024, 1024], P('shard'), may hold values from -0.75 to 0.75
- dense_bias: bfloat16 [1024], P('shard'), may hold values from -4 to 4
- ln2_gain: bfloat16 [1024], P('shard'), may hold values from 0.25 to 1.75
- ln2_bias: bfloat16 [1024], P('shard'), may hold values from -4 to 4
- up_weight: bfloat16 [1024, 4096], P('shard'), may hold values from -0.1875 to 0.1875
- up_bias: bfloat16 [4096], P('shard'), may hold values from -4 to 4
- down_weight: bfloat16 [4096, 1024], P('shard'), may hold values from -0.09375 to 0.09375
- down_bias: bfloat16 [1024], P('shard'), may hold values from -4 to 4
- out_cotangent: bfloat16 [2, 4096, 1024], P('shard', 'ctx'), may hold values from -6 to 6
Outputs:
- block_out: bfloat16 [2, 4096, 1024], P('shard', 'ctx')
- input_grad: bfloat16 [2, 4096, 1024], P('shard', 'ctx')
- ln1_gain_grad: float32 [1024], P('shard')
- ln1_bias_grad: float32 [1024], P('shard')
- qkv_weight_grad: float32 [1024, 3072], P('shard')
- query_bias_grad: float32 [1024], P('shard')
- value_bias_grad: float32 [1024], P('shard')
- dense_weight_grad: float32 [1024, 1024], P('shard')
- dense_bias_grad: float32 [1024], P('shard')
- ln2_gain_grad: float32 [1024], P('shard')
- ln2_bias_grad: float32 [1024], P('shard')
- up_weight_grad: float32 [1024, 4096], P('shard')
- up_bias_grad: float32 [4096], P('shard')
- down_weight_grad: float32 [4096, 1024], P('shard')
- down_bias_grad: float32 [1024], P('shard')
The draws below stay inside these ranges and needn't reach their ends.
All inputs are finite; a program needn't handle non-finite values.
Results may differ from the reference program's by a relative error of at most 0.023.
Values may be sent and summed in bfloat16 or wider, within the bound.
A program may use at most 320 MiB of HBM per device.

```python
import jax
import jax.numpy as jnp
from jax import lax

D = 1024
HEADS = 16
FF = 4096
CTX_TOK = 256
LEN = 4096
SEQS = 2


def level_of(own_key, shape, pieces, smallest, largest):
    gain, own = 1.0, jax.random.fold_in(own_key, 6)
    for position, blocks in pieces:
        heights = jnp.exp(jax.random.uniform(jax.random.fold_in(own, position), (blocks,), jnp.float32, smallest / len(pieces), largest / len(pieces)))
        gain = gain * jnp.repeat(heights, shape[position] // blocks).reshape([-1 if axis == position else 1 for axis in range(len(shape))])
    return gain


def noise(own_key, dims, scale, bound, pieces=(), kind=jnp.bfloat16):
    result = jax.random.normal(own_key, dims, jnp.float32) * scale
    if len(pieces) > 0:
        result = level_of(own_key, dims, pieces, -0.22, 0.18) * result
    return jnp.clip(result, min=-bound, max=bound).astype(kind)


def setup_inputs(seed: int = 0) -> dict:
    key_list = jax.random.split(jax.random.key(seed), 16)
    return {
        "tokens": noise(key_list[0], (SEQS, LEN, D), 1.0, 6.0, ((0, 2), (1, 16))),
        "ln1_gain": jnp.clip(1.0 + 0.15 * jax.random.normal(key_list[1], (D,), jnp.float32), 0.25, 1.75).astype(jnp.bfloat16),
        "ln1_bias": noise(key_list[2], (D,), 0.3, 4.0, ((0, 2),)),
        "qkv_weight": noise(key_list[3], (D, 3 * D), (D // 2) ** -0.5, 0.25, ((0, 2),)),
        "query_bias": noise(key_list[4], (D,), 0.3, 4.0, ((0, 2),)),
        "value_bias": noise(key_list[5], (D,), 0.3, 4.0, ((0, 2),)),
        "dense_weight": noise(key_list[6], (D, D), (D // 16) ** -0.5, 0.75, ((0, 2),)),
        "dense_bias": noise(key_list[7], (D,), 0.3, 4.0, ((0, 2),)),
        "ln2_gain": jnp.clip(1.0 + 0.15 * jax.random.normal(key_list[8], (D,), jnp.float32), 0.25, 1.75).astype(jnp.bfloat16),
        "ln2_bias": noise(key_list[9], (D,), 0.3, 4.0, ((0, 2),)),
        "up_weight": noise(key_list[10], (D, FF), D ** -0.5, 0.1875, ((0, 2),)),
        "up_bias": noise(key_list[11], (FF,), 0.3, 4.0, ((0, 2),)),
        "down_weight": noise(key_list[12], (FF, D), FF ** -0.5, 0.09375, ((0, 2),)),
        "down_bias": noise(key_list[13], (D,), 0.3, 4.0, ((0, 2),)),
        "out_cotangent": noise(key_list[14], (SEQS, LEN, D), 1.0, 6.0, ((0, 2), (1, 16))),
    }


@jax.custom_vjp
def low(v):
    return lax.optimization_barrier(v.astype(jnp.bfloat16)).astype(jnp.float32)

@jax.custom_vjp
def low_back(v):
    return v

def low_keep(v):
    return (low(v), None)

def low_pass(kept, grad):
    return (grad,)

def back_keep(v):
    return (v, None)

def back_low(kept, grad):
    return (low(grad),)
low.defvjp(low_keep, low_pass)
low_back.defvjp(back_keep, back_low)
norm_eps = 1e-05
highest = lax.Precision.HIGHEST

def layer_norm(values, gain_term, bias_term):
    center = values - lax.optimization_barrier(jnp.mean(values, axis=-1, keepdims=True))
    spread = lax.optimization_barrier(jnp.mean(center * center, axis=-1, keepdims=True))
    return center * lax.rsqrt(spread + norm_eps) * gain_term + bias_term

def gelu_tanh(values):
    tanh_input = 0.7978845608028654 * (values + 0.044715 * values * values * values)
    return 0.5 * values * (1.0 + jnp.tanh(tanh_input))

def head_slopes(head_count, block_rows, seq_length):
    head_order = jnp.arange(head_count, dtype=jnp.float32)
    fast_rates = 2.0 ** (-head_order) / (4.0 * block_rows)
    slow_rates = 2.0 / seq_length * 2.0 ** (-(head_order - head_count // 2))
    return jnp.where(head_order < head_count // 2, fast_rates, slow_rates)

def attend(query_heads, key_heads, value_heads, slopes):
    seq_length, head_count, head_dim = query_heads.shape
    block_len = min(512, seq_length)
    key_pos = jnp.arange(seq_length, dtype=jnp.int32)

    def one_block(item):
        query_rows, query_first = item
        query_pos = query_first + jnp.arange(block_len, dtype=jnp.int32)
        raw_scores = jnp.einsum('qhe,khe->hqk', query_rows, key_heads, precision=highest) * head_dim ** (-0.5)
        distance = (key_pos[None, :] - query_pos[:, None]).astype(jnp.float32)
        scores = low_back(raw_scores + slopes[:, None, None] * distance)
        allowed = key_pos[None, :] <= query_pos[:, None]
        weights = low(jax.nn.softmax(jnp.where(allowed, scores, -1e+30), axis=-1))
        return jnp.einsum('hqk,khe->qhe', weights, value_heads, precision=highest)
    block_count = seq_length // block_len
    stacked = lax.map(jax.checkpoint(one_block), (query_heads.reshape(block_count, block_len, head_count, head_dim), jnp.arange(block_count, dtype=jnp.int32) * block_len))
    return stacked.reshape(seq_length, head_count * head_dim)

def layer(params, sequence):
    gain_one, shift_one, weight_qkv, bias_query, bias_value, weight_dense, bias_dense, gain_two, shift_two, weight_up, bias_up, weight_down, bias_down = params
    seq_length, width = sequence.shape
    head_dim = width // HEADS
    normed_one = low(layer_norm(sequence, gain_one, shift_one))
    projected = jnp.dot(normed_one, weight_qkv, precision=highest)
    queries = low_back(low(projected[:, :width] + bias_query))
    key_vals = low_back(low(projected[:, width:2 * width]))
    value_vals = low_back(low(projected[:, 2 * width:] + bias_value))
    attended = attend(queries.reshape(seq_length, HEADS, head_dim), key_vals.reshape(seq_length, HEADS, head_dim), value_vals.reshape(seq_length, HEADS, head_dim), head_slopes(HEADS, CTX_TOK, seq_length))
    attended = low_back(low(attended))
    middle = sequence + low_back(jnp.dot(attended, weight_dense, precision=highest) + bias_dense)
    normed_two = low(layer_norm(middle, gain_two, shift_two))
    hidden = low_back(jnp.dot(normed_two, weight_up, precision=highest) + bias_up)
    active = low(gelu_tanh(hidden))
    return middle + jnp.dot(active, weight_down, precision=highest) + bias_down

def whole(params, inputs):
    return lax.map(lambda sequence: layer(params, sequence), inputs)

def reference(tokens, ln1_gain, ln1_bias, qkv_weight, query_bias, value_bias, dense_weight, dense_bias, ln2_gain, ln2_bias, up_weight, up_bias, down_weight, down_bias, out_cotangent):
    params = (ln1_gain.astype(jnp.float32), ln1_bias.astype(jnp.float32), qkv_weight.astype(jnp.float32), query_bias.astype(jnp.float32), value_bias.astype(jnp.float32), dense_weight.astype(jnp.float32), dense_bias.astype(jnp.float32), ln2_gain.astype(jnp.float32), ln2_bias.astype(jnp.float32), up_weight.astype(jnp.float32), up_bias.astype(jnp.float32), down_weight.astype(jnp.float32), down_bias.astype(jnp.float32))
    inputs = tokens.astype(jnp.float32)
    outputs, pullback = jax.vjp(whole, params, inputs)
    param_grads, input_grad = pullback(out_cotangent.astype(jnp.float32))
    return (outputs.astype(jnp.bfloat16), input_grad.astype(jnp.bfloat16), param_grads[0], param_grads[1], param_grads[2], param_grads[3], param_grads[4], param_grads[5], param_grads[6], param_grads[7], param_grads[8], param_grads[9], param_grads[10], param_grads[11], param_grads[12])
```

```python
import functools

import jax
import jax.numpy as jnp
from jax import lax
from jax.experimental import pallas as pl
from jax.experimental.pallas import tpu as pltpu
from jax.sharding import PartitionSpec as P

HEADS = 16
F32 = jnp.float32
BF = jnp.bfloat16
neg_large = -1e30
norm_eps = 1e-05
VMEM = 48 * 1024 * 1024


def layer_norm(values, gain_term, bias_term):
    center = values - jnp.mean(values, axis=-1, keepdims=True)
    spread = jnp.mean(center * center, axis=-1, keepdims=True)
    return center * lax.rsqrt(spread + norm_eps) * gain_term + bias_term


def gelu_tanh(values):
    tanh_input = 0.7978845608028654 * (values + 0.044715 * values * values * values)
    return 0.5 * values * (1.0 + jnp.tanh(tanh_input))


def dot(a, b):
    return jnp.dot(a, b, preferred_element_type=F32)


def forward_kernel(block, parts, part_ref, k_ref, qt_ref, vt_ref, ot_ref, lse_ref):
    qi = pl.program_id(0)

    def work():
        qt = qt_ref[...]

        def fold(j, carried, masked):
            top, total, acc = carried
            rows = pl.ds(pl.multiple_of(j * block, block), block)
            s = dot(k_ref[rows, :], qt)
            if masked:
                key = lax.broadcasted_iota(jnp.int32, s.shape, 0)
                query = lax.broadcasted_iota(jnp.int32, s.shape, 1)
                s = jnp.where(key <= query, s, neg_large)
            new_top = jnp.maximum(top, jnp.max(s, axis=0, keepdims=True))
            p = jnp.exp(s - new_top)
            factor = jnp.exp(top - new_top)
            total = total * factor + jnp.sum(p, axis=0, keepdims=True)
            acc = acc * factor + dot(vt_ref[:, rows], p.astype(BF))
            return new_top, total, acc

        start = (
            jnp.full((1, block), neg_large, F32),
            jnp.zeros((1, block), F32),
            jnp.zeros((vt_ref.shape[0], block), F32),
        )
        carried = lax.fori_loop(0, qi, lambda j, c: fold(j, c, False), start)
        top, total, acc = fold(qi, carried, True)
        ot_ref[...] = acc / total
        lse_ref[...] = top + jnp.log(total)

    if parts == 1:
        work()
    else:
        mine = qi % parts == part_ref[0]
        pl.when(mine)(work)

        @pl.when(jnp.logical_not(mine))
        def _():
            ot_ref[...] = jnp.zeros_like(ot_ref)
            lse_ref[...] = jnp.zeros_like(lse_ref)


def backward_kernel(
    block, parts, part_ref, k_ref, kt_ref, v_ref, qt_ref, q_ref, dt_ref, d_ref, dq_ref, dkv_ref
):
    ki = pl.program_id(0)
    width = q_ref.shape[1]

    @pl.when(ki == 0)
    def _():
        dq_ref[...] = jnp.zeros_like(dq_ref)

    dkv_ref[...] = jnp.zeros_like(dkv_ref)

    def step(qi, masked):
        cols = pl.ds(pl.multiple_of(qi * block, block), block)
        s = dot(k_ref[...], qt_ref[:, cols])
        if masked:
            key = lax.broadcasted_iota(jnp.int32, s.shape, 0)
            query = lax.broadcasted_iota(jnp.int32, s.shape, 1)
            s = jnp.where(key <= query, s, neg_large)
        p = jnp.exp(s)
        ds = (p * dot(v_ref[...], dt_ref[:, cols])).astype(BF)
        dkv_ref[:, :width] += dot(ds, q_ref[cols, :])
        dkv_ref[:, width:] += dot(p.astype(BF), d_ref[cols, :])
        dq_ref[:, cols] += dot(kt_ref[...], ds)

    def visit(qi, masked):
        if parts == 1:
            step(qi, masked)
        else:
            pl.when(qi % parts == part_ref[0])(lambda: step(qi, masked))

    visit(ki, True)

    def loop(qi, unused):
        visit(qi, False)
        return unused

    lax.fori_loop(ki + 1, q_ref.shape[0] // block, loop, 0)


def split_bf16(row, count):
    terms = []
    for _ in range(count):
        term = row.astype(BF)
        terms.append(term)
        row = row - term.astype(F32)
    return terms


def whole_spec(shape):
    return pl.BlockSpec(shape, lambda i: (0,) * len(shape))


def attention_forward(part, parts, kaug, qtaug, vt):
    length, depth = kaug.shape
    width = vt.shape[0]
    block = min(512, length)
    return pl.pallas_call(
        functools.partial(forward_kernel, block, parts),
        grid=(length // block,),
        in_specs=[
            pl.BlockSpec(memory_space=pltpu.SMEM),
            whole_spec((length, depth)),
            pl.BlockSpec((depth, block), lambda i: (0, i)),
            whole_spec((width, length)),
        ],
        out_specs=[
            pl.BlockSpec((width, block), lambda i: (0, i)),
            pl.BlockSpec((1, block), lambda i: (0, i)),
        ],
        out_shape=[
            jax.ShapeDtypeStruct((width, length), F32),
            jax.ShapeDtypeStruct((1, length), F32),
        ],
        compiler_params=pltpu.CompilerParams(vmem_limit_bytes=VMEM),
        cost_estimate=pl.CostEstimate(
            flops=8 * length * length * width,
            bytes_accessed=8 * length * width,
            transcendentals=length * length // 2,
        ),
        name="attention_forward",
    )(part, kaug, qtaug, vt)


def attention_backward(part, parts, kaug, kt, vaug, qtaug, q, dtaug, d):
    length, depth = kaug.shape
    width = q.shape[1]
    block = min(512, length)
    return pl.pallas_call(
        functools.partial(backward_kernel, block, parts),
        grid=(length // block,),
        in_specs=[
            pl.BlockSpec(memory_space=pltpu.SMEM),
            pl.BlockSpec((block, depth), lambda i: (i, 0)),
            pl.BlockSpec((width, block), lambda i: (0, i)),
            pl.BlockSpec((block, depth), lambda i: (i, 0)),
            whole_spec((depth, length)),
            whole_spec((length, width)),
            whole_spec((depth, length)),
            whole_spec((length, width)),
        ],
        out_specs=[
            whole_spec((width, length)),
            pl.BlockSpec((block, 2 * width), lambda i: (i, 0)),
        ],
        out_shape=[
            jax.ShapeDtypeStruct((width, length), F32),
            jax.ShapeDtypeStruct((length, 2 * width), F32),
        ],
        compiler_params=pltpu.CompilerParams(vmem_limit_bytes=VMEM),
        cost_estimate=pl.CostEstimate(
            flops=24 * length * length * width,
            bytes_accessed=16 * length * width,
            transcendentals=length * length // 2,
        ),
        name="attention_backward",
    )(part, kaug, kt, vaug, qtaug, q, dtaug, d)


def exchange(pick, shard_count):
    me = lax.axis_index("shard")
    out = [(me, pick(me))]
    for k in range(1, shard_count):
        pairs = [(i, (i + k) % shard_count) for i in range(shard_count)]
        out.append(
            (
                (me - k) % shard_count,
                lax.ppermute(pick((me + k) % shard_count), "shard", pairs),
            )
        )
    return out


def stacked(pieces):
    first = pieces[0][1]
    if len(pieces) == 2:
        me, other = pieces[0][0], pieces[1][1]
        low = jnp.where(me == 0, first, other)
        high = jnp.where(me == 0, other, first)
        return jnp.stack([low, high])
    out = jnp.zeros((len(pieces),) + first.shape, first.dtype)
    for source, piece in pieces:
        out = lax.dynamic_update_index_in_dim(out, piece, source, 0)
    return out


def gather(value, shard_count):
    return stacked(exchange(lambda i: value, shard_count))


def at(value, index, axis):
    return lax.dynamic_index_in_dim(value, index, axis, keepdims=False)


def shards(
    tokens,
    ln1_gain,
    ln1_bias,
    qkv_weight,
    query_bias,
    value_bias,
    dense_weight,
    dense_bias,
    ln2_gain,
    ln2_bias,
    up_weight,
    up_bias,
    down_weight,
    down_bias,
    out_cotangent,
):
    n_shard = lax.axis_size("shard")
    n_ctx = lax.axis_size("ctx")
    me = lax.axis_index("shard")
    local_seqs, rows, width = tokens.shape
    seqs = local_seqs * n_shard
    hd = width // HEADS
    heads = HEADS // n_shard
    half = heads * hd
    length = rows * n_ctx
    total = seqs * rows
    ff = up_bias.shape[0]
    pairs = seqs * heads
    parts = n_ctx // pairs
    assert parts * pairs == n_ctx

    small = jnp.stack([ln1_gain, ln1_bias, dense_bias, ln2_gain, ln2_bias, down_bias])
    small = lax.all_gather(small, "shard", axis=1, tiled=True).astype(F32)
    gain1, shift1, bias_dense, gain2, shift2, bias_down = [small[i] for i in range(6)]
    x_low = gather(tokens, n_shard).reshape(total, width)
    qkv_split = qkv_weight.reshape(half, 3, n_shard, half)
    w_qkv = stacked(exchange(lambda i: at(qkv_split, i, 2), n_shard)).reshape(width, 3 * half)
    w_dense = gather(dense_weight, n_shard).reshape(width, width)
    up_split = up_weight.reshape(half, n_shard, ff)
    w_up = stacked(exchange(lambda i: at(up_split, i, 1), n_shard)).reshape(width, ff)
    g_low = gather(out_cotangent, n_shard).reshape(total, width)

    x = x_low.astype(F32)
    h1 = layer_norm(x, gain1, shift1).astype(BF)
    bias_qkv = jnp.concatenate([query_bias, jnp.zeros_like(query_bias), value_bias])
    qkv = (dot(h1, w_qkv) + bias_qkv.astype(F32)).astype(BF)
    send = (
        qkv.reshape(seqs, rows, 3, heads, hd)
        .transpose(0, 3, 2, 4, 1)
        .reshape(pairs, 1, 3 * hd, rows)
    )

    def to_heads(value):
        value = jnp.broadcast_to(value, (pairs, parts) + value.shape[2:])
        value = value.reshape((n_ctx,) + value.shape[2:])
        value = lax.all_to_all(value, "ctx", split_axis=0, concat_axis=0, tiled=True)
        return value.transpose(1, 0, 2).reshape(value.shape[1], length)

    def from_heads(value):
        value = value.reshape(value.shape[0], n_ctx, rows).transpose(1, 0, 2)
        value = lax.all_to_all(value, "ctx", split_axis=0, concat_axis=0, tiled=True)
        value = value.reshape((pairs, parts) + value.shape[1:])
        if parts > 1:
            return jnp.sum(value.astype(F32), axis=1).astype(BF)
        return value[:, 0]

    mine = lax.axis_index("ctx")
    part = (mine % parts).astype(jnp.int32).reshape(1)
    head = me * heads + (mine // parts) % heads
    order = head.astype(F32)
    slope = jnp.where(
        head < HEADS // 2,
        2.0 ** (-order) / (4.0 * rows),
        2.0 / length * 2.0 ** (-(order - HEADS // 2)),
    )
    qkvt = to_heads(send)
    qt, kt, vt = qkvt[:hd], qkvt[hd : 2 * hd], qkvt[2 * hd :]
    scale = hd**-0.5
    place = jnp.arange(length, dtype=jnp.int32)
    far = (slope * (place - place % 256).astype(F32)).astype(BF)[None]
    near = (slope * (place % 256).astype(F32)).astype(BF)[None]
    one = jnp.ones((1, length), BF)
    fill = jnp.zeros((hd - 5, length), BF)
    kaug = jnp.concatenate([kt, far, near, one, one, one, fill]).T
    qs = (qt.astype(F32) * scale).astype(BF)
    zero = jnp.zeros((1, length), BF)
    ot, lse = attention_forward(
        part, parts, kaug, jnp.concatenate([qs, one, one, zero, zero, zero, fill]), vt
    )

    def to_tokens(value, groups):
        return (
            value.reshape(seqs, heads, groups, hd, rows)
            .transpose(0, 4, 2, 1, 3)
            .reshape(total, groups * half)
        )

    attended_half = to_tokens(from_heads(ot.astype(BF)), 1)
    attended = jnp.moveaxis(gather(attended_half, n_shard), 0, 1).reshape(total, width)

    mid = x + dot(attended, w_dense) + bias_dense
    h2 = layer_norm(mid, gain2, shift2).astype(BF)
    hidden = dot(h2, w_up) + up_bias.astype(F32)
    act = gelu_tanh(hidden).astype(BF)
    out_part = dot(act, down_weight).reshape(n_shard, local_seqs, rows, width)
    out_low = out_part.astype(BF)
    received = exchange(lambda i: at(out_low, i, 0), n_shard)[1:]
    own = lambda value: at(value.reshape(n_shard, local_seqs, rows, width), me, 0)
    block_out = own(mid) + at(out_part, me, 0) + bias_down
    for _, piece in received:
        block_out = block_out + piece.astype(F32)
    block_out = block_out.astype(BF)

    g = g_low.astype(F32)
    grad_down = lax.dot_general(act, g_low, (((0,), (0,)), ((), ())), preferred_element_type=F32)
    d_act = lax.dot_general(
        g_low, down_weight, (((1,), (1,)), ((), ())), preferred_element_type=F32
    )
    d_hidden = jax.vjp(gelu_tanh, hidden)[1](d_act)[0].astype(BF)
    d_h2_part = lax.dot_general(
        d_hidden, w_up, (((1,), (1,)), ((), ())), preferred_element_type=F32
    )
    low = d_h2_part.astype(BF)
    d_h2 = d_h2_part
    for _, piece in exchange(lambda i: low, n_shard)[1:]:
        d_h2 = d_h2 + piece.astype(F32)
    grad_up = lax.dot_general(h2, d_hidden, (((0,), (0,)), ((), ())), preferred_element_type=F32)
    d_mid_norm, grad_gain2, grad_shift2 = jax.vjp(layer_norm, mid, gain2, shift2)[1](d_h2)
    d_mid = g + d_mid_norm
    d_dense = d_mid.astype(BF)
    d_attended = lax.dot_general(
        d_dense, dense_weight, (((1,), (1,)), ((), ())), preferred_element_type=F32
    ).astype(BF)
    grad_dense = lax.dot_general(
        attended_half, d_dense, (((0,), (0,)), ((), ())), preferred_element_type=F32
    )

    dt = to_heads(
        d_attended.reshape(seqs, rows, heads, hd)
        .transpose(0, 2, 3, 1)
        .reshape(pairs, 1, hd, rows)
    )
    delta = jnp.sum(dt.astype(F32) * ot, axis=0, keepdims=True)
    qtaug = jnp.concatenate([qs, one, one] + split_bf16(-lse, 3) + [fill])
    dtaug = jnp.concatenate([dt] + split_bf16(-delta, 3) + [jnp.zeros((hd - 3, length), BF)])
    vaug = jnp.concatenate([vt, one, one, one, jnp.zeros((hd - 3, length), BF)]).T
    dqt, dkv = attention_backward(part, parts, kaug, kt, vaug, qtaug, qs.T, dtaug, dt.T)
    d_qkvt = jnp.concatenate([(dqt * scale).astype(BF), dkv.astype(BF).T])
    d_qkv = to_tokens(from_heads(d_qkvt), 3)

    grad_qkv = lax.dot_general(h1, d_qkv, (((0,), (0,)), ((), ())), preferred_element_type=F32)
    d_h1_part = lax.dot_general(d_qkv, w_qkv, (((1,), (1,)), ((), ())), preferred_element_type=F32)
    _, grad_gain1, grad_shift1 = jax.vjp(layer_norm, x, gain1, shift1)[1](d_h1_part)
    d_h1_split = d_h1_part.reshape(n_shard, local_seqs, rows, width)
    d_h1_low = d_h1_split.astype(BF)
    d_h1 = at(d_h1_split, me, 0)
    for _, piece in exchange(lambda i: at(d_h1_low, i, 0), n_shard)[1:]:
        d_h1 = d_h1 + piece.astype(F32)
    d_x = jax.vjp(layer_norm, own(x), gain1, shift1)[1](d_h1)[0]
    input_grad = (own(d_mid) + d_x).astype(BF)

    def column(value, count):
        value = jnp.sum(value.astype(F32), axis=0)
        return lax.dynamic_slice_in_dim(value, me * count, count, 0)

    def piece(value):
        return lax.dynamic_slice_in_dim(value, me * half, half, 0)

    sum_down = lax.psum(grad_down.astype(BF), "ctx")
    sum_up = lax.psum(grad_up.astype(BF), "ctx")
    sum_dense = lax.psum(grad_dense.astype(BF), "ctx")
    sum_down, sum_up, sum_dense, grad_qkv = lax.optimization_barrier(
        (sum_down, sum_up, sum_dense, grad_qkv.astype(BF))
    )
    sum_down, sum_dense = sum_down.astype(F32), sum_dense.astype(F32)
    sum_up = sum_up.reshape(n_shard, half, ff)
    sum_up = stacked(exchange(lambda i: at(sum_up, i, 0), n_shard))
    sum_up = jnp.moveaxis(sum_up, 0, 1).reshape(half, n_shard * ff).astype(F32)
    sum_qkv = lax.psum(grad_qkv, "ctx")
    sum_qkv = sum_qkv.reshape(n_shard, half, 3, half)
    sum_qkv = stacked(exchange(lambda i: at(sum_qkv, i, 0), n_shard))
    sum_qkv = sum_qkv.transpose(1, 2, 0, 3).reshape(half, 3 * width).astype(F32)

    d_qkv_sum = jnp.sum(d_qkv.astype(F32), axis=0)
    early = jnp.concatenate(
        [
            column(g, half),
            jnp.sum(d_hidden.astype(F32), axis=0),
            piece(grad_gain2),
            piece(grad_shift2),
            column(d_dense, half),
        ]
    )
    early = lax.psum(early, "ctx")
    blank = jnp.zeros((width,), F32)
    late = jnp.stack(
        [
            grad_gain1,
            grad_shift1,
            lax.dynamic_update_slice_in_dim(blank, d_qkv_sum[:half], me * half, 0),
            lax.dynamic_update_slice_in_dim(blank, d_qkv_sum[2 * half :], me * half, 0),
        ]
    )
    late = lax.psum(late, ("shard", "ctx"))
    late = lax.dynamic_slice_in_dim(late, me * half, half, 1)
    cut = [half, half + ff, 2 * half + ff, 3 * half + ff]
    down_bias_sum, up_bias_sum, gain2_sum, shift2_sum, dense_bias_sum = jnp.split(early, cut)
    return (
        block_out,
        input_grad,
        late[0],
        late[1],
        sum_qkv,
        late[2],
        late[3],
        sum_dense,
        dense_bias_sum,
        gain2_sum,
        shift2_sum,
        sum_up,
        up_bias_sum,
        sum_down,
        down_bias_sum,
    )


def solution(mesh):
    return jax.shard_map(
        shards,
        mesh=mesh,
        in_specs=(
            P("shard", "ctx", None),
            P("shard"),
            P("shard"),
            P("shard", None),
            P("shard"),
            P("shard"),
            P("shard", None),
            P("shard"),
            P("shard"),
            P("shard"),
            P("shard", None),
            P("shard"),
            P("shard", None),
            P("shard"),
            P("shard", "ctx", None),
        ),
        out_specs=(
            P("shard", "ctx", None),
            P("shard", "ctx", None),
            P("shard"),
            P("shard"),
            P("shard", None),
            P("shard"),
            P("shard"),
            P("shard", None),
            P("shard"),
            P("shard"),
            P("shard"),
            P("shard", None),
            P("shard"),
            P("shard", None),
            P("shard"),
        ),
        check_vma=False,
    )
```
